32 devices in a mesh: graph: 4 (over z), index: 8 (over y, x, core).
Axes of the slice: x: 2, y: 2, z: 4, core: 2. Of those that a mesh axis runs over, the one named last changes fastest.
Arguments:
- features: bfloat16 [8192, 1024], P(('graph', 'index')), may hold values from -6 to 6
- q_weight: bfloat16 [1024, 1024], replicated, may hold values from -0.1875 to 0.1875
- q_bias: float32 [1024], replicated, may hold values from -3 to 3
- w_self: bfloat16 [1024, 1024], replicated, may hold values from -0.125 to 0.125
- w_neigh: bfloat16 [1024, 1024], replicated, may hold values from -0.125 to 0.125
- z_bias: float32 [1024], replicated, may hold values from -3 to 3
- centroids: bfloat16 [2048, 1024], P('index'), may hold values from -0.1875 to 0.1875
- requests: int32 [32, 8, 16], P(('graph', 'index')), may hold values from 0 to 255, as said below
- slots: int32 [8192, 50], P(('graph', 'index')), may hold values from 0 to 127
- importance: float32 [8192, 50], P(('graph', 'index')), may hold values from 0.1 to 10
- labels: int32 [8192, 1], P(('graph', 'index')), may hold values from 0 to 7; in each aligned block of 256 rows (0 to 255, 256 to 511, ...) at most 64 rows name the same one
Outputs:
- scores: bfloat16 [8192, 256], P(('graph', 'index'))
The draws below stay inside these ranges and needn't reach their ends.
Inputs may be any that keep to these rules, and one draw needn't show every extreme that they name: `requests`: the 16 rows that a device asks of one device are distinct. `labels`: the rows of one device carry any one label at most 64 times.
All inputs are finite; a program needn't handle non-finite values.
Results may differ from the reference program's by a relative error of at most 0.0051.
Values may be sent and summed in bfloat16 or wider, within the bound.
A program may use at most 64 MiB of HBM per device.

```python
import math
import jax
import jax.numpy as jnp
import numpy as np
from jax import lax

D = 1024
CENTS = 256
NEIGHBORS = 50
ROWS_DEV = 256
PEERS = 8
SOURCES = 32
FETCH_SLOTS = 16
OWNER_SLOTS = 64
NODES = 8192


def draw_requests(key, part):
    total = SOURCES * PEERS
    keys = jax.random.split(jax.random.fold_in(key, 11), total)
    chosen = jax.random.randint(jax.random.fold_in(key, 12), (), 0, total)
    place = jax.random.randint(jax.random.fold_in(key, 13), (), 0, FETCH_SLOTS)
    flags = jnp.arange(total, dtype=jnp.int32) == chosen

    def one_list(sub_key, forced):
        order = jax.random.permutation(sub_key, ROWS_DEV).astype(jnp.int32)
        where_top = jnp.argmax((order == ROWS_DEV - 1).astype(jnp.int32))
        swapped = order.at[where_top].set(order[place]).at[place].set(ROWS_DEV - 1)
        picked = jnp.where(forced, swapped, order)
        return picked[:FETCH_SLOTS]
    lists = jax.vmap(one_list)(keys, flags)
    return lists.reshape(SOURCES, PEERS, FETCH_SLOTS).astype(jnp.int32)


def place_ends(drawn, stream_key, smallest, largest):
    dims = drawn.shape
    spot = [jax.random.randint(jax.random.fold_in(stream_key, axis), (), 0, dims[axis]) for axis in range(len(dims))]
    drawn = drawn.at[tuple(spot)].set(smallest)
    longest = dims.index(max(dims))
    spot[longest] = (spot[longest] + 1) % dims[longest]
    return drawn.at[tuple(spot)].set(largest)


def levels(own_key, dims, cuts, smallest, largest):
    def one(dim, parts):
        heights = jax.random.uniform(jax.random.fold_in(jax.random.fold_in(own_key, 6), dim), (parts,), jnp.float32, smallest / len(cuts), largest / len(cuts))
        return jnp.repeat(jnp.exp(heights), dims[dim] // parts).reshape((-1,) + (1,) * (len(dims) - dim - 1))

    loudness = one(*cuts[0])
    for cut in cuts[1:]:
        loudness = loudness * one(*cut)
    return loudness


def shared_out(rng, own, number, rows, number_of, top, reach, slope):
    sequence = jax.random.permutation(rng, number_of)
    crowded, usual = load_shares(number_of, rows * top, reach, slope, True), load_shares(number_of, rows * top, reach, slope, False)
    places = jnp.arange(number_of)

    def named(lengths, offset_by):
        used = int((lengths > 0).sum())
        fixed = max(1, used // 4)
        shifted = fixed + (places - fixed + offset_by * (used - fixed)) % max(1, number_of - fixed)
        return jnp.zeros((number_of,), jnp.int32).at[sequence[jnp.where(places < fixed, places, shifted)]].set(jnp.asarray(lengths, jnp.int32))

    lengths = jnp.where(number % 4 == 0, named(crowded, number // 4), named(usual, number - number // 4 - 1))
    mixed = jax.random.permutation(jax.random.fold_in(own, 3), number_of)
    source_of, sink = mixed[0:number_of // 2 * 2:2], mixed[1:number_of // 2 * 2:2]
    margin = jnp.minimum(lengths[source_of] - 1, reach - lengths[sink]) // 2
    margin = jnp.where((source_of == sequence[0]) | (sink == sequence[0]) | (lengths[sink] == 0), 0, jnp.maximum(margin, 0))
    shifted = jax.random.randint(jax.random.fold_in(own, 4), (number_of // 2,), 0, 1 << 20) % (margin + 1)
    lengths = lengths.at[source_of].add(-shifted).at[sink].add(shifted)
    items = jnp.searchsorted(jnp.cumsum(lengths), jnp.arange(rows * top), side="right").astype(jnp.int32)
    grid = items.reshape(top, rows).T
    grid = grid[jax.random.permutation(jax.random.fold_in(own, 1), rows)]
    offset_by = jax.random.randint(jax.random.fold_in(own, 2), (rows, 1), 0, top)
    return jnp.take_along_axis(grid, (jnp.arange(top)[None, :] + offset_by) % top, axis=1)


def load_shares(amount, total, limit, slope, full):
    loads = [(1 << 20) // math.isqrt(rank ** slope) + 1 for rank in range(1, amount + 1)]
    largest = limit if full else min(limit, max(-(-total // amount), total * loads[0] // sum(loads)))
    least = 1 if total - largest >= amount - 1 else 0
    given, surplus = [largest] + [least] * (amount - 1), total - largest - least * (amount - 1)
    while surplus > 0:
        candidates = [i for i in range(1, amount) if given[i] < largest] or [i for i in range(1, amount) if given[i] < limit]
        pool, remaining = sum([loads[i] for i in candidates]), surplus
        for i in candidates:
            more = min(limit - given[i], max(1, remaining * loads[i] // pool), surplus)
            given[i] = given[i] + more
            surplus = surplus - more
    return np.array(given)


def centred(own_key, extent, scale, reach, shards=(), held_as=jnp.bfloat16):
    gain = levels(own_key, extent, shards, -0.22, 0.18) if shards else 1.0
    drawn = jax.random.normal(own_key, extent, jnp.float32) * scale * gain
    return jnp.minimum(jnp.maximum(drawn, -reach), reach).astype(held_as)


def setup_inputs(seed: int = 0) -> dict:
    arg_keys = jax.random.split(jax.random.key(seed), 12)
    features = centred(arg_keys[0], (NODES, D), 1.0, 6.0, ((0, 32),))
    q_weight = centred(arg_keys[1], (D, D), D ** -0.5, 0.1875)
    q_bias = centred(arg_keys[2], (D,), 0.5, 3.0, (), jnp.float32)
    w_self = centred(arg_keys[3], (D, D), (2 * D) ** -0.5, 0.125)
    w_neigh = centred(arg_keys[4], (D, D), (2 * D) ** -0.5, 0.125)
    z_bias = centred(arg_keys[5], (D,), 0.5, 3.0, (), jnp.float32)
    centroids = centred(arg_keys[6], (CENTS * PEERS, D), D ** -0.5, 0.1875, ((0, 8),))
    requests = draw_requests(jax.random.fold_in(arg_keys[11], 71), 0)
    slots = place_ends(jax.random.randint(arg_keys[8], (NODES, NEIGHBORS), 0, PEERS * FETCH_SLOTS), jax.random.fold_in(arg_keys[8], 1), 0, (PEERS * FETCH_SLOTS) - 1).astype(jnp.int32)
    importance = jnp.clip(jnp.exp(math.log(10.0) - 4.6051702 * jax.random.uniform(arg_keys[9], (NODES, NEIGHBORS), jnp.float32) ** levels(arg_keys[9], (NODES, NEIGHBORS), ((0, 32),), -0.2, 0.2)), 0.1, 10.0)
    labels_keys = jax.random.split(jax.random.fold_in(arg_keys[10], 1), NODES // ROWS_DEV)
    labels_turns = jax.random.permutation(jax.random.fold_in(arg_keys[10], 3), NODES // ROWS_DEV)
    labels = jax.vmap(lambda own, number: shared_out(jax.random.fold_in(arg_keys[10], 2), own, number, ROWS_DEV, PEERS, 1, OWNER_SLOTS, 2))(labels_keys, labels_turns).reshape((NODES, 1))
    return {"features": features, "q_weight": q_weight, "q_bias": q_bias, "w_self": w_self, "w_neigh": w_neigh, "z_bias": z_bias, "centroids": centroids, "requests": requests, "slots": slots, "importance": importance, "labels": labels}


def place_rows(label_rows):
    hits = (label_rows[:, None] == jnp.arange(PEERS, dtype=jnp.int32)[None, :]).astype(jnp.int32)
    ranks = lax.optimization_barrier(jnp.sum(hits * (jnp.cumsum(hits, axis=0) - 1), axis=1))
    return label_rows * OWNER_SLOTS + ranks

def pool_device(device, messages, requests, slots, weights_norm):
    group_id = device // PEERS
    asked_rows = requests[device]
    owner_ids = group_id * PEERS + jnp.arange(PEERS, dtype=jnp.int32)
    global_rows = (owner_ids[:, None] * ROWS_DEV + asked_rows).reshape(-1)
    fetched = jnp.take(messages, global_rows, axis=0)
    slot_rows = lax.dynamic_slice_in_dim(slots, device * ROWS_DEV, ROWS_DEV, 0)
    weight_rows = lax.dynamic_slice_in_dim(weights_norm, device * ROWS_DEV, ROWS_DEV, 0)
    slot_ids = jnp.arange(PEERS * FETCH_SLOTS, dtype=jnp.int32)
    mixing = lax.optimization_barrier(jnp.sum(jnp.where(slot_rows[:, :, None] == slot_ids[None, None, :], weight_rows[:, :, None], 0.0), axis=1)).astype(jnp.bfloat16)
    return jnp.dot(mixing, fetched, preferred_element_type=jnp.float32).astype(jnp.bfloat16)

def score_device(device, normed, labels, blocks):
    row_block = lax.dynamic_slice_in_dim(normed, device * ROWS_DEV, ROWS_DEV, 0)
    label_rows = lax.dynamic_slice_in_dim(labels, device * ROWS_DEV, ROWS_DEV, 0)[:, 0]
    positions = place_rows(label_rows)
    buffer = jnp.zeros((PEERS * OWNER_SLOTS, normed.shape[1]), normed.dtype).at[positions].set(row_block)
    buffer = buffer.reshape(PEERS, OWNER_SLOTS, normed.shape[1]).astype(jnp.float32)
    raw = jnp.einsum('pcd,pkd->pck', buffer, blocks).astype(jnp.bfloat16)
    return jnp.take(raw.reshape(PEERS * OWNER_SLOTS, CENTS), positions, axis=0)

def reference(features, q_weight, q_bias, w_self, w_neigh, z_bias, centroids, requests, slots, importance, labels):
    width = features.shape[1]
    messages = jax.nn.relu(jnp.dot(features, q_weight, preferred_element_type=jnp.float32) + q_bias).astype(jnp.bfloat16)
    weights_norm = importance / lax.optimization_barrier(jnp.sum(importance, axis=1, keepdims=True))
    device_ids = jnp.arange(SOURCES, dtype=jnp.int32)
    pooled = lax.map(lambda device: pool_device(device, messages, requests, slots, weights_norm), device_ids).reshape(-1, width)
    hidden = jax.nn.relu(jnp.dot(features, w_self, preferred_element_type=jnp.float32) + jnp.dot(pooled, w_neigh, preferred_element_type=jnp.float32) + z_bias)
    normed = (hidden * lax.rsqrt(lax.optimization_barrier(jnp.mean(hidden * hidden, axis=1, keepdims=True)) + 1e-06)).astype(jnp.bfloat16)
    blocks = centroids.astype(jnp.float32).reshape(PEERS, CENTS, width)
    scores = lax.map(lambda device: score_device(device, normed, labels, blocks), device_ids)
    return scores.reshape(-1, CENTS)
```

```python
import functools

import jax
import jax.numpy as jnp
from jax import lax
from jax.experimental import pallas as pl
from jax.experimental.pallas import tpu as pltpu
from jax.sharding import PartitionSpec as P

MESH = pl.DeviceIdType.MESH
LANES = 128
TILE = 256


def chip_bits(peers):
    return [1 << k for k in range(1, peers.bit_length() - 1)]


def even_offsets(peers):
    return sorted(range(2, peers, 2), key=lambda d: (bin(d).count("1"), d))


def kernel(
    graphs,
    peers,
    features_hbm,
    q_weight_hbm,
    q_bias_hbm,
    w_self_hbm,
    w_neigh_hbm,
    z_bias_hbm,
    centroids_hbm,
    requests_hbm,
    slots_hbm,
    importance_hbm,
    labels_hbm,
    out_ref,
    features,
    q_weight,
    q_bias,
    w_self,
    w_neigh,
    z_bias,
    shards,
    requests,
    slots,
    importance,
    labels,
    asked,
    rows_out,
    rows_in,
    mixing,
    pooled,
    hidden,
    squares,
    normed,
    total,
    load_sems,
    send_sems,
    main_sems,
    side_sems,
    asked_sems,
    rows_sems,
):
    graph = lax.axis_index("graph")
    me = lax.axis_index("index")
    row_count, width = features.shape
    cents = shards.shape[1]
    fetch = requests.shape[1]
    slot_count = peers * fetch
    bits = chip_bits(peers)

    def flip(value, bit):
        return value + bit * (1 - 2 * ((value // bit) % 2))

    def at_offset(offset):
        value = me
        bit = 1
        while bit < peers:
            if offset & bit:
                value = flip(value, bit)
            bit *= 2
        return value

    role = graph % 2
    across = flip(graph, 1)

    share = cents * 5 // 16 // 16 * 16
    common = cents - 2 * share
    share_a = (share // 2 + 15) // 16 * 16
    common_a = (common // 2 + 15) // 16 * 16

    def rows_of(part):
        start, size = {
            0: (role * share, share_a),
            1: (role * share + share_a, share - share_a),
            2: (2 * share, common_a),
            3: (2 * share + common_a, common - common_a),
            4: ((1 - role) * share, share_a),
            5: ((1 - role) * share + share_a, share - share_a),
        }[part]
        return pl.ds(start if isinstance(start, int) else pl.multiple_of(start, 16), size)

    loads = []
    for source, target in (
        (requests_hbm, requests),
        (features_hbm, features),
        (centroids_hbm, shards.at[me]),
        (slots_hbm, slots),
        (importance_hbm, importance),
        (w_self_hbm, w_self),
        (z_bias_hbm, z_bias),
        (q_weight_hbm, q_weight),
        (q_bias_hbm, q_bias),
        (w_neigh_hbm, w_neigh),
        (labels_hbm, labels),
    ):
        load = pltpu.make_async_copy(source, target, load_sems.at[len(loads)])
        load.start()
        loads.append(load)

    barrier = pltpu.get_barrier_semaphore()
    for offset in range(1, peers):
        pl.semaphore_signal(barrier, inc=1, device_id=(graph, at_offset(offset)), device_id_type=MESH)
    pl.semaphore_signal(barrier, inc=1, device_id=(across, me), device_id_type=MESH)
    pl.semaphore_wait(barrier, peers)

    sent = []

    def send(source, target, arrival, device):
        copy = pltpu.make_async_remote_copy(
            src_ref=source,
            dst_ref=target,
            send_sem=send_sems.at[len(sent)],
            recv_sem=arrival,
            device_id=device,
            device_id_type=MESH,
        )
        copy.start()
        sent.append(copy)

    def await_arrival(target, arrival):
        pltpu.make_async_remote_copy(
            src_ref=target,
            dst_ref=target,
            send_sem=send_sems.at[0],
            recv_sem=arrival,
            device_id=(graph, at_offset(1)),
            device_id_type=MESH,
        ).wait_recv()

    def part_ref(offset, part):
        return shards.at[at_offset(offset), rows_of(part)]

    def send_on(offset, part, bit):
        ref = part_ref(offset, part)
        send(ref, ref, main_sems.at[(offset | bit) // 2, part], (graph, flip(me, bit)))

    def relay(offset, part):
        ref = part_ref(offset, part)
        await_arrival(ref, main_sems.at[offset // 2, part])
        if part in (0, 2):
            for bit in bits:
                if bit > offset:
                    send_on(offset, part, bit)
        elif part in (1, 3):
            for bit in bits:
                if bit < (offset & -offset):
                    send_on(offset, part, bit)
        if part in (0, 1):
            send(ref, ref, main_sems.at[offset // 2, part + 4], (across, me))
        send(ref, ref, side_sems.at[offset // 2, part], (graph, flip(me, 1)))

    loads[0].wait()
    for offset in range(1, peers):
        peer = at_offset(offset)
        send(requests.at[peer], asked.at[me], asked_sems.at[offset], (graph, peer))
    asked[pl.ds(me, 1)] = requests[pl.ds(me, 1)]

    loads[2].wait()
    for part in (0, 1):
        for bit in bits:
            send_on(0, part, bit)
    send(shards.at[me], shards.at[me], side_sems.at[0, 0], (graph, flip(me, 1)))

    loads[1].wait()
    for offset in range(1, peers):
        await_arrival(asked.at[at_offset(offset)], asked_sems.at[offset])
    wanted = asked[...].reshape(slot_count, LANES)
    lane = lax.broadcasted_iota(jnp.int32, (slot_count, LANES), 1)
    chosen = jnp.concatenate(
        [jnp.where(wanted == lane + first, 1.0, 0.0) for first in range(0, row_count, LANES)], axis=1
    ).astype(jnp.bfloat16)

    @pl.loop(0, width // TILE)
    def _(step):
        cols = pl.ds(pl.multiple_of(step * TILE, TILE), TILE)
        rows_out[:, :, cols] = (
            jnp.dot(chosen, features[:, cols], preferred_element_type=jnp.float32)
            .astype(jnp.bfloat16)
            .reshape(peers, fetch, TILE)
        )

    for offset in range(1, peers):
        peer = at_offset(offset)
        send(rows_out.at[peer], rows_in.at[me], rows_sems.at[offset], (graph, peer))
    rows_in[pl.ds(me, 1)] = rows_out[pl.ds(me, 1)]
    for part in (2, 3):
        for bit in bits:
            send_on(0, part, bit)

    loads[3].wait()
    loads[4].wait()
    block = 64

    @pl.loop(0, row_count // block)
    def _(step):
        rows = pl.ds(pl.multiple_of(step * block, block), block)
        raw = importance[rows, :]
        scaled = raw / jnp.sum(raw, axis=1, keepdims=True)
        places = slots[rows, :]
        ids = lax.broadcasted_iota(jnp.int32, (block, slot_count), 1)
        mix = jnp.zeros((block, slot_count), jnp.float32)
        for k in range(raw.shape[1]):
            mix = mix + jnp.where(places[:, k : k + 1] == ids, scaled[:, k : k + 1], 0.0)
        mixing[rows, :] = mix.astype(jnp.bfloat16)

    offsets = even_offsets(peers)
    single = [d for d in offsets if d in bits]
    several = [d for d in offsets if d not in bits]
    for d in single:
        relay(d, 0)
        relay(d, 1)

    loads[5].wait()
    loads[6].wait()

    @pl.loop(0, width // TILE)
    def _(step):
        cols = pl.ds(pl.multiple_of(step * TILE, TILE), TILE)
        hidden[:, cols] = (
            jnp.dot(features[...], w_self[:, cols], preferred_element_type=jnp.float32) + z_bias[:, cols]
        )

    loads[7].wait()
    loads[8].wait()
    for offset in range(1, peers):
        await_arrival(rows_in.at[at_offset(offset)], rows_sems.at[offset])

    @pl.loop(0, width // TILE)
    def _(step):
        cols = pl.ds(pl.multiple_of(step * TILE, TILE), TILE)
        message = jnp.maximum(
            jnp.dot(
                rows_in[...].reshape(slot_count, width),
                q_weight[:, cols],
                preferred_element_type=jnp.float32,
            )
            + q_bias[:, cols],
            0.0,
        ).astype(jnp.bfloat16)
        pooled[:, cols] = jnp.dot(mixing[...], message, preferred_element_type=jnp.float32).astype(
            jnp.bfloat16
        )

    for d in single:
        relay(d, 2)
        relay(d, 3)
    loads[9].wait()
    squares[...] = jnp.zeros_like(squares)

    @pl.loop(0, width // TILE)
    def _(step):
        cols = pl.ds(pl.multiple_of(step * TILE, TILE), TILE)
        part = jnp.maximum(
            hidden[:, cols] + jnp.dot(pooled[...], w_neigh[:, cols], preferred_element_type=jnp.float32),
            0.0,
        )
        hidden[:, cols] = part
        for first in range(0, TILE, LANES):
            piece = part[:, first : first + LANES]
            squares[...] += piece * piece

    inverse = lax.rsqrt(jnp.sum(squares[...], axis=1, keepdims=True) / width + 1e-06)
    normed[...] = (hidden[...] * inverse).astype(jnp.bfloat16)

    for part in (0, 1, 2, 3):
        for d in several:
            relay(d, part)

    loads[10].wait()

    def score(offset):
        shard = at_offset(offset)
        scores = lax.dot_general(
            normed[...], shards[shard], (((1,), (1,)), ((), ())), preferred_element_type=jnp.float32
        )
        total[...] = scores if offset == 0 else jnp.where(labels[...] == shard, scores, total[...])

    score(0)
    await_arrival(shards.at[at_offset(1)], side_sems.at[0, 0])
    score(1)
    for d in offsets:
        relay(d, 4)
        relay(d, 5)
        score(d)
    for d in offsets:
        for part in range(6):
            ref = part_ref(d ^ 1, part)
            await_arrival(ref, side_sems.at[d // 2, part])
        score(d ^ 1)
    out_ref[...] = total[...].astype(out_ref.dtype)
    for copy in sent:
        copy.wait_send()


def body(
    graphs,
    peers,
    features,
    q_weight,
    q_bias,
    w_self,
    w_neigh,
    z_bias,
    centroids,
    requests,
    slots,
    importance,
    labels,
):
    rows, width = features.shape
    cents = centroids.shape[0]
    fetch = requests.shape[2]
    slot_count = peers * fetch
    wide = jnp.broadcast_to(requests[0][:, :, None], (peers, fetch, LANES))
    far = peers // 2 - 1
    sends = 12 * far + len(chip_bits(peers)) * 4 + 1 + 2 * (peers - 1)
    bf16, f32, i32 = jnp.bfloat16, jnp.float32, jnp.int32
    dma = pltpu.SemaphoreType.DMA
    flops = 2 * rows * width * (3 * width + peers * cents)
    return pl.pallas_call(
        functools.partial(kernel, graphs, peers),
        out_shape=jax.ShapeDtypeStruct((rows, cents), bf16),
        in_specs=[pl.BlockSpec(memory_space=pl.ANY)] * 11,
        out_specs=pl.BlockSpec(memory_space=pltpu.VMEM),
        scratch_shapes=[
            pltpu.VMEM((rows, width), bf16),
            pltpu.VMEM((width, width), bf16),
            pltpu.VMEM((1, width), f32),
            pltpu.VMEM((width, width), bf16),
            pltpu.VMEM((width, width), bf16),
            pltpu.VMEM((1, width), f32),
            pltpu.VMEM((peers, cents, width), bf16),
            pltpu.VMEM((peers, fetch, LANES), i32),
            pltpu.VMEM(slots.shape, i32),
            pltpu.VMEM(importance.shape, f32),
            pltpu.VMEM(labels.shape, i32),
            pltpu.VMEM((peers, fetch, LANES), i32),
            pltpu.VMEM((peers, fetch, width), bf16),
            pltpu.VMEM((peers, fetch, width), bf16),
            pltpu.VMEM((rows, slot_count), bf16),
            pltpu.VMEM((rows, width), bf16),
            pltpu.VMEM((rows, width), f32),
            pltpu.VMEM((rows, LANES), f32),
            pltpu.VMEM((rows, width), bf16),
            pltpu.VMEM((rows, cents), f32),
            dma((11,)),
            dma((sends,)),
            dma((peers // 2, 6)),
            dma((peers // 2, 6)),
            dma((peers,)),
            dma((peers,)),
        ],
        compiler_params=pltpu.CompilerParams(
            collective_id=0, has_side_effects=True, vmem_limit_bytes=48 * 1024 * 1024
        ),
        cost_estimate=pl.CostEstimate(flops=flops, bytes_accessed=8 * 1024 * 1024, transcendentals=rows),
    )(
        features,
        q_weight,
        q_bias.reshape(1, -1),
        w_self,
        w_neigh,
        z_bias.reshape(1, -1),
        centroids,
        wide,
        slots,
        importance,
        labels,
    )


def solution(mesh):
    return jax.shard_map(
        functools.partial(body, mesh.shape["graph"], mesh.shape["index"]),
        mesh=mesh,
        in_specs=(
            P(("graph", "index"), None),
            P(),
            P(),
            P(),
            P(),
            P(),
            P("index", None),
            P(("graph", "index"), None, None),
            P(("graph", "index"), None),
            P(("graph", "index"), None),
            P(("graph", "index"), None),
        ),
        out_specs=P(("graph", "index"), None),
        check_vma=False,
    )
```

```python
import functools

import jax
import jax.numpy as jnp
from jax import lax
from jax.experimental import pallas as pl
from jax.experimental.pallas import tpu as pltpu
from jax.sharding import PartitionSpec as P

MESH = pl.DeviceIdType.MESH
LANES = 128
TILE = 256


def chip_bits(peers):
    return [1 << k for k in range(1, peers.bit_length() - 1)]


def even_offsets(peers):
    return sorted(range(2, peers, 2), key=lambda d: (bin(d).count("1"), d))


def kernel(
    graphs,
    peers,
    features_hbm,
    q_weight_hbm,
    q_bias_hbm,
    w_self_hbm,
    w_neigh_hbm,
    z_bias_hbm,
    centroids_hbm,
    requests_hbm,
    slots_hbm,
    importance_hbm,
    labels_hbm,
    out_ref,
    features,
    q_weight,
    q_bias,
    w_self,
    w_neigh,
    z_bias,
    shards,
    requests,
    slots,
    importance,
    labels,
    label_rows,
    asked,
    rows_out,
    rows_in,
    mixing,
    pooled,
    hidden,
    squares,
    normed,
    total,
    load_sems,
    send_sems,
    main_sems,
    side_sems,
    asked_sems,
    rows_sems,
):
    graph = lax.axis_index("graph")
    me = lax.axis_index("index")
    row_count, width = features.shape
    cents = shards.shape[1]
    fetch = rows_in.shape[1]
    slot_count = peers * fetch
    bits = chip_bits(peers)

    def flip(value, bit):
        return value + bit * (1 - 2 * ((value // bit) % 2))

    def at_offset(offset):
        value = me
        bit = 1
        while bit < peers:
            if offset & bit:
                value = flip(value, bit)
            bit *= 2
        return value

    role = graph % 2
    across = flip(graph, 1)

    share = cents * 5 // 16 // 16 * 16
    common = cents - 2 * share
    share_a = (share // 2 + 15) // 16 * 16
    common_a = (common // 2 + 15) // 16 * 16

    def rows_of(part):
        start, size = {
            0: (role * share, share_a),
            1: (role * share + share_a, share - share_a),
            2: (2 * share, common_a),
            3: (2 * share + common_a, common - common_a),
            4: ((1 - role) * share, share_a),
            5: ((1 - role) * share + share_a, share - share_a),
        }[part]
        return pl.ds(start if isinstance(start, int) else pl.multiple_of(start, 16), size)

    loads = []
    for source, target in (
        (requests_hbm, requests),
        (features_hbm, features),
        (centroids_hbm, shards.at[me]),
        (slots_hbm, slots),
        (importance_hbm, importance),
        (w_self_hbm, w_self),
        (z_bias_hbm, z_bias),
        (q_weight_hbm, q_weight),
        (q_bias_hbm, q_bias),
        (w_neigh_hbm, w_neigh),
        (labels_hbm, labels),
    ):
        load = pltpu.make_async_copy(source, target, load_sems.at[len(loads)])
        load.start()
        loads.append(load)

    barrier = pltpu.get_barrier_semaphore()
    for offset in range(1, peers):
        pl.semaphore_signal(barrier, inc=1, device_id=(graph, at_offset(offset)), device_id_type=MESH)
    pl.semaphore_signal(barrier, inc=1, device_id=(across, me), device_id_type=MESH)
    pl.semaphore_wait(barrier, peers)

    sent = []

    def send(source, target, arrival, device):
        copy = pltpu.make_async_remote_copy(
            src_ref=source,
            dst_ref=target,
            send_sem=send_sems.at[len(sent)],
            recv_sem=arrival,
            device_id=device,
            device_id_type=MESH,
        )
        copy.start()
        sent.append(copy)

    def await_arrival(target, arrival):
        pltpu.make_async_remote_copy(
            src_ref=target,
            dst_ref=target,
            send_sem=send_sems.at[0],
            recv_sem=arrival,
            device_id=(graph, at_offset(1)),
            device_id_type=MESH,
        ).wait_recv()

    def part_ref(offset, part):
        return shards.at[at_offset(offset), rows_of(part)]

    def send_on(offset, part, bit):
        ref = part_ref(offset, part)
        send(ref, ref, main_sems.at[(offset | bit) // 2, part], (graph, flip(me, bit)))

    def relay(offset, part):
        ref = part_ref(offset, part)
        await_arrival(ref, main_sems.at[offset // 2, part])
        if part in (0, 2):
            for bit in bits:
                if bit > offset:
                    send_on(offset, part, bit)
        elif part in (1, 3):
            for bit in bits:
                if bit < (offset & -offset):
                    send_on(offset, part, bit)
        if part in (0, 1):
            send(ref, ref, main_sems.at[offset // 2, part + 4], (across, me))
        send(ref, ref, side_sems.at[offset // 2, part], (graph, flip(me, 1)))

    loads[0].wait()
    for offset in range(1, peers):
        peer = at_offset(offset)
        send(requests, asked.at[me], asked_sems.at[offset], (graph, peer))
    asked[pl.ds(me, 1)] = requests[...][None]

    loads[2].wait()
    for part in (0, 1):
        for bit in bits:
            send_on(0, part, bit)
    send(shards.at[me], shards.at[me], side_sems.at[0, 0], (graph, flip(me, 1)))

    loads[1].wait()
    for offset in range(1, peers):
        await_arrival(asked.at[at_offset(offset)], asked_sems.at[offset])
    lists = jnp.concatenate(
        [jnp.broadcast_to(asked[p, pl.ds(me, 1), :], (fetch, fetch)) for p in range(peers)], axis=0
    )
    own = lax.broadcasted_iota(jnp.int32, (slot_count, fetch), 0) % fetch
    turn = lax.broadcasted_iota(jnp.int32, (slot_count, fetch), 1)
    wanted = jnp.sum(jnp.where(own == turn, lists, 0).astype(jnp.float32), axis=1, keepdims=True)
    ids = lax.broadcasted_iota(jnp.int32, (slot_count, row_count), 1).astype(jnp.float32)
    chosen = jnp.where(wanted == ids, 1.0, 0.0).astype(jnp.bfloat16)

    @pl.loop(0, width // TILE)
    def _(step):
        cols = pl.ds(pl.multiple_of(step * TILE, TILE), TILE)
        rows_out[:, :, cols] = (
            jnp.dot(chosen, features[:, cols], preferred_element_type=jnp.float32)
            .astype(jnp.bfloat16)
            .reshape(peers, fetch, TILE)
        )

    for offset in range(1, peers):
        peer = at_offset(offset)
        send(rows_out.at[peer], rows_in.at[me], rows_sems.at[offset], (graph, peer))
    rows_in[pl.ds(me, 1)] = rows_out[pl.ds(me, 1)]
    for part in (2, 3):
        for bit in bits:
            send_on(0, part, bit)

    loads[3].wait()
    loads[4].wait()
    block = 128

    @pl.loop(0, row_count // block)
    def _(step):
        rows = pl.ds(pl.multiple_of(step * block, block), block)
        scaled = importance[:, rows] / jnp.sum(importance[:, rows], axis=0, keepdims=True)
        places = slots[:, rows]
        for first in range(0, slot_count, LANES):
            ids = lax.broadcasted_iota(jnp.int32, (LANES, block), 0) + first
            mix = jnp.zeros((LANES, block), jnp.float32)
            for k in range(places.shape[0]):
                mix = mix + jnp.where(places[k : k + 1, :] == ids, scaled[k : k + 1, :], 0.0)
            mixing[rows, first : first + LANES] = mix.T.astype(jnp.bfloat16)

    offsets = even_offsets(peers)
    single = [d for d in offsets if d in bits]
    several = [d for d in offsets if d not in bits]
    for d in single:
        relay(d, 0)
        relay(d, 1)

    loads[5].wait()
    loads[6].wait()

    @pl.loop(0, width // TILE)
    def _(step):
        cols = pl.ds(pl.multiple_of(step * TILE, TILE), TILE)
        hidden[:, cols] = (
            jnp.dot(features[...], w_self[:, cols], preferred_element_type=jnp.float32) + z_bias[:, cols]
        )

    loads[7].wait()
    loads[8].wait()
    for offset in range(1, peers):
        await_arrival(rows_in.at[at_offset(offset)], rows_sems.at[offset])

    @pl.loop(0, width // TILE)
    def _(step):
        cols = pl.ds(pl.multiple_of(step * TILE, TILE), TILE)
        message = jnp.maximum(
            jnp.dot(
                rows_in[...].reshape(slot_count, width),
                q_weight[:, cols],
                preferred_element_type=jnp.float32,
            )
            + q_bias[:, cols],
            0.0,
        ).astype(jnp.bfloat16)
        pooled[:, cols] = jnp.dot(mixing[...], message, preferred_element_type=jnp.float32).astype(
            jnp.bfloat16
        )

    for d in single:
        relay(d, 2)
        relay(d, 3)
    loads[9].wait()
    squares[...] = jnp.zeros_like(squares)

    @pl.loop(0, width // TILE)
    def _(step):
        cols = pl.ds(pl.multiple_of(step * TILE, TILE), TILE)
        part = jnp.maximum(
            hidden[:, cols] + jnp.dot(pooled[...], w_neigh[:, cols], preferred_element_type=jnp.float32),
            0.0,
        )
        hidden[:, cols] = part
        for first in range(0, TILE, LANES):
            piece = part[:, first : first + LANES]
            squares[...] += piece * piece

    inverse = lax.rsqrt(jnp.sum(squares[...], axis=1, keepdims=True) / width + 1e-06)
    normed[...] = (hidden[...] * inverse).astype(jnp.bfloat16)

    for part in (0, 1, 2, 3):
        for d in several:
            relay(d, part)

    loads[10].wait()
    label_rows[...] = jnp.broadcast_to(labels[...], (LANES, row_count)).T

    def score(offset):
        shard = at_offset(offset)
        scores = lax.dot_general(
            normed[...], shards[shard], (((1,), (1,)), ((), ())), preferred_element_type=jnp.float32
        )
        total[...] = scores if offset == 0 else jnp.where(
            jnp.concatenate([label_rows[...]] * (cents // LANES), axis=1) == shard, scores, total[...]
        )

    score(0)
    await_arrival(shards.at[at_offset(1)], side_sems.at[0, 0])
    score(1)
    for d in offsets:
        relay(d, 4)
        relay(d, 5)
        score(d)
    for d in offsets:
        for part in range(6):
            ref = part_ref(d ^ 1, part)
            await_arrival(ref, side_sems.at[d // 2, part])
        score(d ^ 1)
    out_ref[...] = total[...].astype(out_ref.dtype)
    for copy in sent:
        copy.wait_send()


def body(
    graphs,
    peers,
    features,
    q_weight,
    q_bias,
    w_self,
    w_neigh,
    z_bias,
    centroids,
    requests,
    slots,
    importance,
    labels,
):
    rows, width = features.shape
    cents = centroids.shape[0]
    fetch = requests.shape[2]
    slot_count = peers * fetch
    far = peers // 2 - 1
    sends = 12 * far + len(chip_bits(peers)) * 4 + 1 + 2 * (peers - 1)
    bf16, f32, i32 = jnp.bfloat16, jnp.float32, jnp.int32
    dma = pltpu.SemaphoreType.DMA
    flops = 2 * rows * width * (3 * width + peers * cents)
    return pl.pallas_call(
        functools.partial(kernel, graphs, peers),
        out_shape=jax.ShapeDtypeStruct((rows, cents), bf16),
        in_specs=[pl.BlockSpec(memory_space=pltpu.HBM)] * 11,
        out_specs=pl.BlockSpec(memory_space=pltpu.VMEM),
        scratch_shapes=[
            pltpu.VMEM((rows, width), bf16),
            pltpu.VMEM((width, width), bf16),
            pltpu.VMEM((1, width), f32),
            pltpu.VMEM((width, width), bf16),
            pltpu.VMEM((width, width), bf16),
            pltpu.VMEM((1, width), f32),
            pltpu.VMEM((peers, cents, width), bf16),
            pltpu.VMEM((peers, fetch), i32),
            pltpu.VMEM(slots.shape[::-1], i32),
            pltpu.VMEM(importance.shape[::-1], f32),
            pltpu.VMEM((1, rows), i32),
            pltpu.VMEM((rows, LANES), i32),
            pltpu.VMEM((peers, peers, fetch), i32),
            pltpu.VMEM((peers, fetch, width), bf16),
            pltpu.VMEM((peers, fetch, width), bf16),
            pltpu.VMEM((rows, slot_count), bf16),
            pltpu.VMEM((rows, width), bf16),
            pltpu.VMEM((rows, width), f32),
            pltpu.VMEM((rows, LANES), f32),
            pltpu.VMEM((rows, width), bf16),
            pltpu.VMEM((rows, cents), f32),
            dma((11,)),
            dma((sends,)),
            dma((peers // 2, 6)),
            dma((peers // 2, 6)),
            dma((peers,)),
            dma((peers,)),
        ],
        compiler_params=pltpu.CompilerParams(
            collective_id=0, has_side_effects=True, vmem_limit_bytes=58 * 1024 * 1024
        ),
        cost_estimate=pl.CostEstimate(flops=flops, bytes_accessed=8 * 1024 * 1024, transcendentals=rows),
    )(
        features,
        q_weight,
        q_bias.reshape(1, -1),
        w_self,
        w_neigh,
        z_bias.reshape(1, -1),
        centroids,
        requests[0],
        slots.T,
        importance.T,
        labels.reshape(1, -1),
    )


def solution(mesh):
    return jax.shard_map(
        functools.partial(body, mesh.shape["graph"], mesh.shape["index"]),
        mesh=mesh,
        in_specs=(
            P(("graph", "index"), None),
            P(),
            P(),
            P(),
            P(),
            P(),
            P("index", None),
            P(("graph", "index"), None, None),
            P(("graph", "index"), None),
            P(("graph", "index"), None),
            P(("graph", "index"), None),
        ),
        out_specs=P(("graph", "index"), None),
        check_vma=False,
    )
```

```python
import functools

import jax
import jax.numpy as jnp
from jax import lax
from jax.experimental import pallas as pl
from jax.experimental.pallas import tpu as pltpu
from jax.sharding import PartitionSpec as P

MESH = pl.DeviceIdType.MESH
LANES = 128
TILE = 256
CHUNKS = 2


def chip_bits(peers):
    return [1 << k for k in range(1, peers.bit_length() - 1)]


def even_offsets(peers):
    return sorted(range(2, peers, 2), key=lambda d: (bin(d).count("1"), d))


def kernel(
    graphs,
    peers,
    features_hbm,
    q_weight_hbm,
    q_bias_hbm,
    w_self_hbm,
    w_neigh_hbm,
    z_bias_hbm,
    centroids_hbm,
    requests_hbm,
    slots_hbm,
    importance_hbm,
    labels_hbm,
    out_ref,
    features,
    q_weight,
    q_bias,
    w_self,
    w_neigh,
    z_bias,
    shards,
    requests,
    slots,
    importance,
    labels,
    label_rows,
    asked,
    rows_out,
    rows_in,
    mixing,
    pooled,
    hidden,
    squares,
    normed,
    total,
    load_sems,
    send_sems,
    main_sems,
    side_sems,
    asked_sems,
    rows_sems,
):
    graph = lax.axis_index("graph")
    me = lax.axis_index("index")
    row_count, width = features.shape
    cents = shards.shape[1]
    fetch = rows_in.shape[1]
    slot_count = peers * fetch
    bits = chip_bits(peers)

    def flip(value, bit):
        return value + bit * (1 - 2 * ((value // bit) % 2))

    def at_offset(offset):
        value = me
        bit = 1
        while bit < peers:
            if offset & bit:
                value = flip(value, bit)
            bit *= 2
        return value

    role = graph % 2
    across = flip(graph, 1)

    half = cents // 2
    size = half // CHUNKS
    top = bits[-1]

    def rows_of(part):
        first = role if part < CHUNKS else 1 - role
        return pl.ds(pl.multiple_of(first * half + part % CHUNKS * size, 16), size)

    def onward(offset, part):
        if part < CHUNKS:
            return [bit for bit in bits if bit > offset and offset | bit != top]
        low = offset & -offset if offset else 2 * top
        return [bit for bit in bits if bit < low and offset | bit != bits[0]]

    loads = []
    for source, target in (
        (requests_hbm, requests),
        (features_hbm, features),
        (centroids_hbm, shards.at[me]),
        (slots_hbm, slots),
        (importance_hbm, importance),
        (w_self_hbm, w_self),
        (z_bias_hbm, z_bias),
        (q_weight_hbm, q_weight),
        (q_bias_hbm, q_bias),
        (w_neigh_hbm, w_neigh),
        (labels_hbm, labels),
    ):
        load = pltpu.make_async_copy(source, target, load_sems.at[len(loads)])
        load.start()
        loads.append(load)

    barrier = pltpu.get_barrier_semaphore()
    for offset in range(1, peers):
        pl.semaphore_signal(barrier, inc=1, device_id=(graph, at_offset(offset)), device_id_type=MESH)
    pl.semaphore_signal(barrier, inc=1, device_id=(across, me), device_id_type=MESH)
    pl.semaphore_wait(barrier, peers)

    sent = []

    def send(source, target, arrival, device):
        copy = pltpu.make_async_remote_copy(
            src_ref=source,
            dst_ref=target,
            send_sem=send_sems.at[len(sent)],
            recv_sem=arrival,
            device_id=device,
            device_id_type=MESH,
        )
        copy.start()
        sent.append(copy)

    def await_arrival(target, arrival):
        pltpu.make_async_remote_copy(
            src_ref=target,
            dst_ref=target,
            send_sem=send_sems.at[0],
            recv_sem=arrival,
            device_id=(graph, at_offset(1)),
            device_id_type=MESH,
        ).wait_recv()

    def part_ref(offset, part):
        return shards.at[at_offset(offset), rows_of(part)]

    def send_on(offset, part, bit):
        ref = part_ref(offset, part)
        send(ref, ref, main_sems.at[(offset | bit) // 2, part], (graph, flip(me, bit)))

    def relay(offset, part):
        ref = part_ref(offset, part)
        await_arrival(ref, main_sems.at[offset // 2, part])
        for bit in onward(offset, part):
            send_on(offset, part, bit)
        if (offset == bits[0] and part < CHUNKS) or (offset == top and part >= CHUNKS):
            other = (part + CHUNKS) % (2 * CHUNKS)
            send(ref, ref, main_sems.at[offset // 2, other], (across, me))
        send(ref, ref, side_sems.at[offset // 2, part], (graph, flip(me, 1)))

    loads[0].wait()
    for offset in range(1, peers):
        peer = at_offset(offset)
        send(requests, asked.at[me], asked_sems.at[offset], (graph, peer))
    asked[pl.ds(me, 1)] = requests[...][None]

    loads[2].wait()
    for chunk in range(CHUNKS):
        for part in (chunk, chunk + CHUNKS):
            for bit in onward(0, part):
                send_on(0, part, bit)
    send(shards.at[me], shards.at[me], side_sems.at[0, 0], (graph, flip(me, 1)))

    loads[3].wait()
    loads[4].wait()
    block = 128

    @pl.loop(0, row_count // block)
    def _(step):
        rows = pl.ds(pl.multiple_of(step * block, block), block)
        scaled = importance[:, rows] / jnp.sum(importance[:, rows], axis=0, keepdims=True)
        places = slots[:, rows]
        for first in range(0, slot_count, LANES):
            ids = lax.broadcasted_iota(jnp.int32, (LANES, block), 0) + first
            mix = jnp.zeros((LANES, block), jnp.float32)
            for k in range(places.shape[0]):
                mix = mix + jnp.where(places[k : k + 1, :] == ids, scaled[k : k + 1, :], 0.0)
            mixing[rows, first : first + LANES] = mix.T.astype(jnp.bfloat16)

    by_tree = [(d, part) for d in even_offsets(peers) for part in range(2 * CHUNKS)]
    by_layer = [(bits[0], part + CHUNKS) for part in range(CHUNKS)] + [(top, part) for part in range(CHUNKS)]
    by_tree = [event for event in by_tree if event not in by_layer]
    rounds = []
    for late in (False, True):
        for chunk in range(CHUNKS):
            events = [e for e in by_tree if (e[0] not in bits) == late and e[1] % CHUNKS == chunk]
            events += [e for e in by_layer if late and e[1] % CHUNKS == chunk]
            rounds.append(events)

    def relay_rounds(count):
        for events in rounds[:count]:
            for offset, part in events:
                relay(offset, part)
        del rounds[:count]

    relay_rounds(CHUNKS // 2)

    loads[1].wait()
    for offset in range(1, peers):
        await_arrival(asked.at[at_offset(offset)], asked_sems.at[offset])
    lists = jnp.concatenate(
        [jnp.broadcast_to(asked[p, pl.ds(me, 1), :], (fetch, fetch)) for p in range(peers)], axis=0
    )
    own = lax.broadcasted_iota(jnp.int32, (slot_count, fetch), 0) % fetch
    turn = lax.broadcasted_iota(jnp.int32, (slot_count, fetch), 1)
    wanted = jnp.sum(jnp.where(own == turn, lists, 0).astype(jnp.float32), axis=1, keepdims=True)
    ids = lax.broadcasted_iota(jnp.int32, (slot_count, row_count), 1).astype(jnp.float32)
    chosen = jnp.where(wanted == ids, 1.0, 0.0).astype(jnp.bfloat16)

    @pl.loop(0, width // TILE)
    def _(step):
        cols = pl.ds(pl.multiple_of(step * TILE, TILE), TILE)
        rows_out[:, :, cols] = (
            jnp.dot(chosen, features[:, cols], preferred_element_type=jnp.float32)
            .astype(jnp.bfloat16)
            .reshape(peers, fetch, TILE)
        )

    for offset in range(1, peers):
        peer = at_offset(offset)
        send(rows_out.at[peer], rows_in.at[me], rows_sems.at[offset], (graph, peer))
    rows_in[pl.ds(me, 1)] = rows_out[pl.ds(me, 1)]

    relay_rounds(CHUNKS // 2)

    loads[5].wait()
    loads[6].wait()

    @pl.loop(0, width // TILE)
    def _(step):
        cols = pl.ds(pl.multiple_of(step * TILE, TILE), TILE)
        hidden[:, cols] = (
            jnp.dot(features[...], w_self[:, cols], preferred_element_type=jnp.float32) + z_bias[:, cols]
        )

    loads[7].wait()
    loads[8].wait()
    for offset in range(1, peers):
        await_arrival(rows_in.at[at_offset(offset)], rows_sems.at[offset])

    @pl.loop(0, width // TILE)
    def _(step):
        cols = pl.ds(pl.multiple_of(step * TILE, TILE), TILE)
        message = jnp.maximum(
            jnp.dot(
                rows_in[...].reshape(slot_count, width),
                q_weight[:, cols],
                preferred_element_type=jnp.float32,
            )
            + q_bias[:, cols],
            0.0,
        ).astype(jnp.bfloat16)
        pooled[:, cols] = jnp.dot(mixing[...], message, preferred_element_type=jnp.float32).astype(
            jnp.bfloat16
        )

    relay_rounds(CHUNKS // 2)
    loads[9].wait()
    squares[...] = jnp.zeros_like(squares)

    @pl.loop(0, width // TILE)
    def _(step):
        cols = pl.ds(pl.multiple_of(step * TILE, TILE), TILE)
        part = jnp.maximum(
            hidden[:, cols] + jnp.dot(pooled[...], w_neigh[:, cols], preferred_element_type=jnp.float32),
            0.0,
        )
        hidden[:, cols] = part
        for first in range(0, TILE, LANES):
            piece = part[:, first : first + LANES]
            squares[...] += piece * piece

    inverse = lax.rsqrt(jnp.sum(squares[...], axis=1, keepdims=True) / width + 1e-06)
    normed[...] = (hidden[...] * inverse).astype(jnp.bfloat16)

    loads[10].wait()
    label_rows[...] = jnp.broadcast_to(labels[...], (LANES, row_count)).T
    same = jnp.concatenate([label_rows[...]] * (half // LANES), axis=1)

    def dots(block):
        return lax.dot_general(
            normed[...], block, (((1,), (1,)), ((), ())), preferred_element_type=jnp.float32
        )

    def score(offset):
        shard = at_offset(offset)
        scores = dots(shards[shard])
        if offset == 0:
            total[...] = scores
        else:
            total[...] = jnp.where(jnp.concatenate([same, same], axis=1) == shard, scores, total[...])

    def score_halves(low, high, first):
        parts = ((at_offset(low), first), (at_offset(high), 1 - first))
        spans = [pl.ds(pl.multiple_of(which * half, half), half) for _, which in parts]
        scores = dots(
            jnp.concatenate([shards[shard, span, :] for (shard, _), span in zip(parts, spans)], axis=0)
        )
        for place, ((shard, _), span) in enumerate(zip(parts, spans)):
            piece = scores[:, place * half : (place + 1) * half]
            total[:, span] = jnp.where(same == shard, piece, total[:, span])

    def await_side(offset, parts):
        for part in parts:
            await_arrival(part_ref(offset ^ 1, part), side_sems.at[offset // 2, part])

    ahead, behind = range(CHUNKS), range(CHUNKS, 2 * CHUNKS)
    relay_rounds(CHUNKS // 2)
    score(0)
    await_arrival(shards.at[at_offset(1)], side_sems.at[0, 0])
    score(1)
    relay_rounds(CHUNKS // 4)
    score_halves(bits[0], top, role)
    await_side(bits[0], ahead)
    await_side(top, behind)
    score_halves(bits[0] ^ 1, top ^ 1, role)
    relay_rounds(2 * CHUNKS)
    score_halves(bits[0], top, 1 - role)
    others = [d for d in even_offsets(peers) if d not in (bits[0], top)]
    for d in others:
        score(d)
    await_side(bits[0], behind)
    await_side(top, ahead)
    score_halves(bits[0] ^ 1, top ^ 1, 1 - role)
    for d in others:
        await_side(d, range(2 * CHUNKS))
        score(d ^ 1)
    out_ref[...] = total[...].astype(out_ref.dtype)
    for copy in sent:
        copy.wait_send()


def body(
    graphs,
    peers,
    features,
    q_weight,
    q_bias,
    w_self,
    w_neigh,
    z_bias,
    centroids,
    requests,
    slots,
    importance,
    labels,
):
    rows, width = features.shape
    cents = centroids.shape[0]
    fetch = requests.shape[2]
    slot_count = peers * fetch
    far = peers // 2 - 1
    sends = 4 * CHUNKS * far + 1 + 2 * (peers - 1)
    bf16, f32, i32 = jnp.bfloat16, jnp.float32, jnp.int32
    dma = pltpu.SemaphoreType.DMA
    flops = 2 * rows * width * (3 * width + peers * cents)
    return pl.pallas_call(
        functools.partial(kernel, graphs, peers),
        out_shape=jax.ShapeDtypeStruct((rows, cents), bf16),
        in_specs=[pl.BlockSpec(memory_space=pltpu.HBM)] * 11,
        out_specs=pl.BlockSpec(memory_space=pltpu.VMEM),
        scratch_shapes=[
            pltpu.VMEM((rows, width), bf16),
            pltpu.VMEM((width, width), bf16),
            pltpu.VMEM((1, width), f32),
            pltpu.VMEM((width, width), bf16),
            pltpu.VMEM((width, width), bf16),
            pltpu.VMEM((1, width), f32),
            pltpu.VMEM((peers, cents, width), bf16),
            pltpu.VMEM((peers, fetch), i32),
            pltpu.VMEM(slots.shape[::-1], i32),
            pltpu.VMEM(importance.shape[::-1], f32),
            pltpu.VMEM((1, rows), i32),
            pltpu.VMEM((rows, LANES), i32),
            pltpu.VMEM((peers, peers, fetch), i32),
            pltpu.VMEM((peers, fetch, width), bf16),
            pltpu.VMEM((peers, fetch, width), bf16),
            pltpu.VMEM((rows, slot_count), bf16),
            pltpu.VMEM((rows, width), bf16),
            pltpu.VMEM((rows, width), f32),
            pltpu.VMEM((rows, LANES), f32),
            pltpu.VMEM((rows, width), bf16),
            pltpu.VMEM((rows, cents), f32),
            dma((11,)),
            dma((sends,)),
            dma((peers // 2, 2 * CHUNKS)),
            dma((peers // 2, 2 * CHUNKS)),
            dma((peers,)),
            dma((peers,)),
        ],
        compiler_params=pltpu.CompilerParams(
            collective_id=0, has_side_effects=True, vmem_limit_bytes=58 * 1024 * 1024
        ),
        cost_estimate=pl.CostEstimate(flops=flops, bytes_accessed=8 * 1024 * 1024, transcendentals=rows),
    )(
        features,
        q_weight,
        q_bias.reshape(1, -1),
        w_self,
        w_neigh,
        z_bias.reshape(1, -1),
        centroids,
        requests[0],
        slots.T,
        importance.T,
        labels.reshape(1, -1),
    )


def solution(mesh):
    return jax.shard_map(
        functools.partial(body, mesh.shape["graph"], mesh.shape["index"]),
        mesh=mesh,
        in_specs=(
            P(("graph", "index"), None),
            P(),
            P(),
            P(),
            P(),
            P(),
            P("index", None),
            P(("graph", "index"), None, None),
            P(("graph", "index"), None),
            P(("graph", "index"), None),
            P(("graph", "index"), None),
        ),
        out_specs=P(("graph", "index"), None),
        check_vma=False,
    )
```
